32 devices in a mesh: stream: 2 (over y), seq: 8 (over z, core), tensor: 2 (over x).
Axes of the slice: x: 2, y: 2, z: 4, core: 2. Of those that a mesh axis runs over, the one named last changes fastest.
Arguments:
- hidden: bfloat16 [2, 1, 4096, 4096], P('stream', None, 'seq', 'tensor'), may hold values from -32 to 32
- norm_gain: float32 [4096], replicated, may hold values from 0.1 to 1.9
- query_weight: bfloat16 [4096, 4096], P('seq', 'tensor'), may hold values from -1 to 1
- key_weight: bfloat16 [4096, 1024], P('seq', 'tensor'), may hold values from -24 to 24
- value_projection_weight: bfloat16 [4096, 1024], P('seq', 'tensor'), may hold values from -0.09375 to 0.09375
- out_weight: bfloat16 [4096, 4096], P('tensor', 'seq'), may hold values from -0.125 to 0.125
Outputs:
- cross_out: bfloat16 [2, 1, 4096, 4096], P('stream', None, 'seq', 'tensor')
The draws below stay inside these ranges and needn't reach their ends.
All inputs are finite; a program needn't handle non-finite values.
Results may differ from the reference program's by a relative error of at most 0.014.
The reference program's roundings to bfloat16 on the way count: a program that leaves them out, or rounds other values in their place, can miss the bound.
Values may be sent and summed in bfloat16 or wider, within the bound.
A program may use at most 256 MiB of HBM per device.

```python
import math
import jax
import jax.numpy as jnp
from jax import lax

MODEL_DIM = 4096
QUERY_HEAD_COUNT = 32
KV_HEAD_COUNT = 8
HEAD_DIM = 128
WINDOW_BATCH = 1
FRAME_LENGTH = 4096
N_TENSOR = 2


def draw_hidden(key, part):
    random_subkeys = jax.random.split(jax.random.fold_in(key, 3), 4)
    full_shape = (2, WINDOW_BATCH, FRAME_LENGTH, MODEL_DIM)
    raw_field = jnp.clip(jax.random.normal(random_subkeys[0], full_shape, jnp.float32), -4.0, 4.0)
    lower_log = math.log(0.5)
    upper_log = math.log(2.0)
    feature = jnp.exp(jax.random.uniform(random_subkeys[2], (MODEL_DIM,), jnp.float32, lower_log, upper_log))
    row_scale = jnp.exp(jax.random.uniform(random_subkeys[3], (2, WINDOW_BATCH, FRAME_LENGTH, 1), jnp.float32, lower_log, upper_log))
    hidden_field = raw_field * feature * row_scale
    return hidden_field.astype(jnp.bfloat16)


def weight_pair(key):
    random_subkeys = jax.random.split(jax.random.fold_in(key, 17), 3)
    query_projection_matrix = jnp.clip(jax.random.normal(random_subkeys[0], (MODEL_DIM, QUERY_HEAD_COUNT * HEAD_DIM), jnp.float32), -6.0, 6.0) * MODEL_DIM ** (-0.5)
    cross_scale = jnp.exp(jax.random.uniform(random_subkeys[2], (KV_HEAD_COUNT,), jnp.float32, math.log(1.5), math.log(4.0)))
    unnormed_keys = jnp.clip(jax.random.normal(random_subkeys[1], (MODEL_DIM, KV_HEAD_COUNT, HEAD_DIM), jnp.float32), -6.0, 6.0) * MODEL_DIM ** (-0.5)
    key_projection_matrix = (unnormed_keys * cross_scale[None, :, None]).reshape(MODEL_DIM, KV_HEAD_COUNT * HEAD_DIM)
    return (query_projection_matrix, key_projection_matrix)


def draw_query_weight(key, part):
    return weight_pair(key)[0].astype(jnp.bfloat16)


def draw_key_weight(key, part):
    return weight_pair(key)[1].astype(jnp.bfloat16)


def spiked(array, rng, source, target, shards_of, factor):
    owner, partner = [(jnp.arange(array.shape[axis_at]) // (array.shape[axis_at] // shards_of)).reshape([-1 if axis == axis_at else 1 for axis in range(array.ndim)]) for axis_at in (source, target)]
    chosen = jax.random.permutation(rng, shards_of)[partner]
    strong = (owner == chosen) | (owner == (partner + shards_of // 2) % shards_of)
    return jnp.where(strong, factor * array, array)


def block_levels(rng, dims, cuts, smallest, high):
    factor_of = 1.0
    for position, blocks in cuts:
        steps = jax.random.uniform(jax.random.fold_in(jax.random.fold_in(rng, 6), position), (blocks,), jnp.float32, smallest / len(cuts), high / len(cuts))
        factor_of = factor_of * jnp.repeat(jnp.exp(steps), dims[position] // blocks).reshape((-1,) + (1,) * (len(dims) - 1 - position))
    return factor_of


def normal_values(rng, extent, spread, reach, cuts=(), kind=jnp.bfloat16):
    entries = jax.random.normal(rng, extent, jnp.float32) * spread
    if len(cuts) > 0:
        entries = block_levels(rng, extent, cuts, -0.22, 0.18) * entries
    return jnp.clip(entries, min=-reach, max=reach).astype(kind)


def heavy_noise(key, dims, deviation, bound, shards, heavy, held_as=jnp.bfloat16):
    values = deviation * jax.random.normal(key, dims, jnp.float32)
    if shards:
        values = values * block_levels(key, dims, shards, -0.22, 0.18)
    return jnp.clip(spiked(values, jax.random.fold_in(key, 3), *heavy), -bound, bound).astype(held_as)


def setup_inputs(seed: int = 0) -> dict:
    streams_of = jax.random.split(jax.random.key(seed), 7)
    return {
        "hidden": draw_hidden(jax.random.fold_in(streams_of[6], 71), 0),
        "norm_gain": jnp.clip(1.0 + 0.18 * jax.random.normal(streams_of[1], (MODEL_DIM,), jnp.float32), 0.1, 1.9),
        "query_weight": draw_query_weight(jax.random.fold_in(streams_of[6], 71), 0),
        "key_weight": draw_key_weight(jax.random.fold_in(streams_of[6], 71), 0),
        "value_projection_weight": normal_values(streams_of[4], (MODEL_DIM, KV_HEAD_COUNT * HEAD_DIM), MODEL_DIM ** -0.5, 0.09375, ((0, 8), (1, 2))),
        "out_weight": heavy_noise(streams_of[5], (QUERY_HEAD_COUNT * HEAD_DIM, MODEL_DIM), (QUERY_HEAD_COUNT * HEAD_DIM) ** -0.5, 0.125, ((0, 2), (1, 8)), (0, 1, 8, 2.0)),
    }


def reference(hidden, norm_gain, query_weight, key_weight, value_projection_weight, out_weight):
    group_repeat = QUERY_HEAD_COUNT // KV_HEAD_COUNT
    widened = hidden.astype(jnp.float32)
    inverse_rms = lax.rsqrt(lax.optimization_barrier(jnp.mean(widened * widened, axis=-1, keepdims=True)) + 1e-05)
    normed = (widened * inverse_rms * norm_gain).astype(jnp.bfloat16)
    flattened = normed.reshape(-1, MODEL_DIM)
    query_rows = jnp.dot(flattened, query_weight, preferred_element_type=jnp.float32).astype(jnp.bfloat16)
    self_key_rows = jnp.dot(flattened, key_weight, preferred_element_type=jnp.float32).astype(jnp.bfloat16)
    self_value_rows = jnp.dot(flattened, value_projection_weight, preferred_element_type=jnp.float32).astype(jnp.bfloat16)
    query_rows = query_rows.reshape(2, WINDOW_BATCH, FRAME_LENGTH, KV_HEAD_COUNT, group_repeat, HEAD_DIM)
    self_key_rows = self_key_rows.reshape(2, WINDOW_BATCH, FRAME_LENGTH, KV_HEAD_COUNT, HEAD_DIM)[::-1]
    self_value_rows = self_value_rows.reshape(2, WINDOW_BATCH, FRAME_LENGTH, KV_HEAD_COUNT, HEAD_DIM)[::-1]
    query_groups = query_rows.transpose(0, 1, 3, 2, 4, 5).reshape(-1, FRAME_LENGTH, group_repeat, HEAD_DIM)
    key_groups = self_key_rows.transpose(0, 1, 3, 2, 4).reshape(-1, FRAME_LENGTH, HEAD_DIM)
    value_groups = self_value_rows.transpose(0, 1, 3, 2, 4).reshape(-1, FRAME_LENGTH, HEAD_DIM)
    positions = jnp.arange(FRAME_LENGTH, dtype=jnp.int32)
    allowed = positions[None, :] <= positions[:, None]

    def one_group(operands):
        query_tile, key_tile, value_tile = operands
        scores = jnp.einsum('frd,gd->rfg', query_tile.astype(jnp.float32), key_tile.astype(jnp.float32)) * HEAD_DIM ** (-0.5)
        scores = jnp.where(allowed[None], scores, -1e+30)
        row_max = lax.optimization_barrier(jnp.max(scores, axis=-1, keepdims=True))
        expo = jnp.where(allowed[None], jnp.exp(scores - row_max), 0.0)
        totals = lax.optimization_barrier(jnp.sum(expo, axis=-1, keepdims=True))
        weights = lax.optimization_barrier(expo.astype(jnp.bfloat16))
        attended_output = jnp.einsum('rfg,gd->rfd', weights.astype(jnp.float32), value_tile.astype(jnp.float32)) / totals
        return attended_output.astype(jnp.bfloat16)
    attended_output = lax.map(one_group, (query_groups, key_groups, value_groups))
    attended_output = attended_output.reshape(2, WINDOW_BATCH, KV_HEAD_COUNT, group_repeat, FRAME_LENGTH, HEAD_DIM).transpose(0, 1, 4, 2, 3, 5)
    attended_output = attended_output.reshape(2 * WINDOW_BATCH * FRAME_LENGTH, QUERY_HEAD_COUNT * HEAD_DIM)
    group_width = QUERY_HEAD_COUNT * HEAD_DIM // N_TENSOR

    def add_share(index, total):
        start = (index * group_width).astype(jnp.int32)
        columns = lax.dynamic_slice_in_dim(attended_output, start, group_width, 1)
        rows = lax.dynamic_slice_in_dim(out_weight, start, group_width, 0)
        share = jnp.dot(columns, rows, preferred_element_type=jnp.float32).astype(jnp.bfloat16)
        share = lax.optimization_barrier(share)
        return total + share.astype(jnp.float32)
    initial = jnp.zeros((2 * WINDOW_BATCH * FRAME_LENGTH, MODEL_DIM), jnp.float32)
    summed = lax.fori_loop(jnp.int32(0), jnp.int32(N_TENSOR), add_share, initial)
    return summed.astype(jnp.bfloat16).reshape(2, WINDOW_BATCH, FRAME_LENGTH, MODEL_DIM)
```

```python
import functools

import jax
import jax.numpy as jnp
from jax import lax
from jax.experimental import pallas as pl
from jax.experimental.pallas import tpu as pltpu
from jax.sharding import PartitionSpec as P

HEAD_DIM = 128
ROW_CHUNKS = 2
KEY_BLOCK = 512
LOG2E = 1.4426950408889634


def swap_pairs(block, axis):
    count = lax.axis_size(axis)
    return lax.ppermute(block, axis, [(i, i ^ 1) for i in range(count)])


def attend_kernel(repeat, start_ref, q_ref, k_ref, v_ref, o_ref, m_ref, l_ref, acc_ref):
    step = pl.program_id(1)
    rows = q_ref.shape[0]
    keys = k_ref.shape[0]
    start = start_ref[0]
    last = (start + rows - 1) // keys
    scale = LOG2E * HEAD_DIM ** (-0.5)

    @pl.when(step == 0)
    def _():
        m_ref[...] = jnp.full_like(m_ref, -1e30)
        l_ref[...] = jnp.zeros_like(l_ref)
        acc_ref[...] = jnp.zeros_like(acc_ref)

    def update(masked):
        k = k_ref[...]
        v = v_ref[...]
        if masked:
            frame = start + lax.broadcasted_iota(jnp.int32, (rows, keys), 0)
            key = step * keys + lax.broadcasted_iota(jnp.int32, (rows, keys), 1)
            allowed = key <= frame
        for r in range(repeat):
            q = q_ref[:, r * HEAD_DIM:(r + 1) * HEAD_DIM]
            s = lax.dot_general(q, k, (((1,), (1,)), ((), ())), preferred_element_type=jnp.float32)
            if masked:
                s = jnp.where(allowed, s, -1e30)
            top = jnp.max(s, axis=1, keepdims=True) * scale
            before = m_ref[r]
            fresh = jnp.maximum(before, top)
            m_ref[r] = fresh
            alpha = jnp.exp2(before - fresh)
            p = jnp.exp2(s * scale - fresh[:, :1])
            part = p[:, :HEAD_DIM]
            for j in range(1, keys // HEAD_DIM):
                part = part + p[:, j * HEAD_DIM:(j + 1) * HEAD_DIM]
            l_ref[r] = alpha * l_ref[r] + part
            acc_ref[r] = alpha * acc_ref[r] + jnp.dot(
                p.astype(jnp.bfloat16), v, preferred_element_type=jnp.float32
            )

    @pl.when(step < last)
    def _():
        update(False)

    @pl.when(step == last)
    def _():
        update(True)
        for r in range(repeat):
            totals = jnp.sum(l_ref[r], axis=1, keepdims=True)
            o_ref[:, r * HEAD_DIM:(r + 1) * HEAD_DIM] = (acc_ref[r] / totals).astype(o_ref.dtype)


def attend(start, queries, keys_values, repeat):
    rows, width = queries.shape
    count = keys_values.shape[0]
    groups = width // (repeat * HEAD_DIM)
    block = min(KEY_BLOCK, count)

    def at(step, start_ref):
        return jnp.minimum(step, (start_ref[0] + rows - 1) // block)

    return pl.pallas_call(
        functools.partial(attend_kernel, repeat),
        out_shape=jax.ShapeDtypeStruct((rows, width), jnp.bfloat16),
        grid_spec=pltpu.PrefetchScalarGridSpec(
            num_scalar_prefetch=1,
            grid=(groups, count // block),
            in_specs=[
                pl.BlockSpec((rows, repeat * HEAD_DIM), lambda g, i, s: (0, g)),
                pl.BlockSpec((block, HEAD_DIM), lambda g, i, s: (at(i, s), g)),
                pl.BlockSpec((block, HEAD_DIM), lambda g, i, s: (at(i, s), groups + g)),
            ],
            out_specs=pl.BlockSpec((rows, repeat * HEAD_DIM), lambda g, i, s: (0, g)),
            scratch_shapes=[
                pltpu.VMEM((repeat, rows, HEAD_DIM), jnp.float32),
                pltpu.VMEM((repeat, rows, HEAD_DIM), jnp.float32),
                pltpu.VMEM((repeat, rows, HEAD_DIM), jnp.float32),
            ],
        ),
        compiler_params=pltpu.CompilerParams(
            dimension_semantics=("arbitrary", "arbitrary"), vmem_limit_bytes=32 * 1024 * 1024
        ),
        cost_estimate=pl.CostEstimate(
            flops=8 * rows * count * width,
            bytes_accessed=2 * (2 * rows * width + keys_values.size),
            transcendentals=rows * count * width // HEAD_DIM,
        ),
    )(start.reshape(1), queries, keys_values, keys_values)


def y_share(mine, core):
    depth = mine.shape[0] // 2
    part = lax.dynamic_slice_in_dim(mine, core * depth, depth, 0)
    near = lax.ppermute(part, "stream", [(0, 1), (1, 0)])
    far = swap_pairs(near, "seq")
    return near, far


def body(hidden, norm_gain, query_weight, key_weight, value_projection_weight, out_weight):
    windows, frame_count = hidden.shape[1], hidden.shape[2]
    n_tensor = lax.axis_size("tensor")
    n_seq = lax.axis_size("seq")
    stream = lax.axis_index("stream")
    tensor = lax.axis_index("tensor")
    seq = lax.axis_index("seq")
    core = seq % 2
    rows = windows * frame_count
    depth = query_weight.shape[0] // 2
    out_half = out_weight.shape[1] // 2

    kv_weight = jnp.concatenate([key_weight, value_projection_weight], axis=1)
    kv_mine = lax.all_gather(
        lax.dynamic_slice_in_dim(kv_weight, stream * depth, depth, 0), "seq", axis=0, tiled=True
    )
    query_half, kv_mine = lax.optimization_barrier(
        (lax.dynamic_slice_in_dim(query_weight, stream * depth, depth, 0), kv_mine)
    )
    query_mine = lax.all_gather(query_half, "seq", axis=0, tiled=True)
    out_piece, query_mine = lax.optimization_barrier(
        (lax.dynamic_slice_in_dim(out_weight, stream * out_half, out_half, 1), query_mine)
    )
    out_mine = lax.all_gather(out_piece, "seq", axis=1, tiled=True)

    local = hidden.reshape(rows, hidden.shape[3])
    if n_tensor == 2:
        other = lax.ppermute(local, "tensor", [(0, 1), (1, 0)])
        gathered = jnp.where(
            tensor == 0,
            jnp.concatenate([local, other], axis=1),
            jnp.concatenate([other, local], axis=1),
        )
    else:
        gathered = lax.all_gather(local, "tensor", axis=1, tiled=True)
    flat = gathered.astype(jnp.float32)
    inverse_rms = lax.rsqrt(jnp.mean(flat * flat, axis=1, keepdims=True) + 1e-05)
    normed = (flat * inverse_rms * norm_gain).astype(jnp.bfloat16)
    split = normed.reshape(rows, n_seq, 2, depth)

    def features(half):
        return lax.dynamic_index_in_dim(split, half, 2, keepdims=False).reshape(rows, n_seq * depth)

    normed_mine = features(stream)
    normed_other = features(1 - stream)
    span = n_seq * depth // 2
    normed_near = lax.dynamic_slice_in_dim(normed_other, core * span, span, 1)
    normed_far = lax.dynamic_slice_in_dim(normed_other, (1 - core) * span, span, 1)

    def project(mine, near, far):
        total = jnp.dot(normed_mine, mine, preferred_element_type=jnp.float32)
        total += jnp.dot(normed_near, near, preferred_element_type=jnp.float32)
        total += jnp.dot(normed_far, far, preferred_element_type=jnp.float32)
        return total.astype(jnp.bfloat16)

    keys_values = project(kv_mine, *y_share(kv_mine, core))
    partner = lax.ppermute(keys_values, "stream", [(0, 1), (1, 0)])
    partner, out_mine = lax.optimization_barrier((partner, out_mine))
    pieces = lax.all_gather(
        partner.reshape(windows, frame_count, partner.shape[1]), "seq", axis=1, tiled=True
    )
    queries = project(query_mine, *y_share(query_mine, core)).reshape(windows, frame_count, -1)
    out_near, out_far = y_share(out_mine, core)
    width = out_weight.shape[0] // 2

    repeat = query_weight.shape[1] // key_weight.shape[1]
    chunk = frame_count // ROW_CHUNKS

    def scattered(share):
        if n_tensor == 2:
            wide = share.shape[1] // 2
            away = lax.dynamic_slice_in_dim(share, (1 - tensor) * wide, wide, 1)
            kept = lax.dynamic_slice_in_dim(share, tensor * wide, wide, 1)
            came = lax.ppermute(away, "tensor", [(0, 1), (1, 0)])
            return (kept.astype(jnp.float32) + came.astype(jnp.float32)).astype(jnp.bfloat16)
        return lax.psum_scatter(share, "tensor", scatter_dimension=1, tiled=True)

    outs = []
    for window in range(windows):
        for index in range(ROW_CHUNKS):
            start = seq * frame_count + index * chunk
            attended = attend(
                start,
                lax.slice_in_dim(queries[window], index * chunk, (index + 1) * chunk, axis=0),
                pieces[window],
                repeat,
            )
            share_mine = jnp.dot(attended, out_mine, preferred_element_type=jnp.float32)
            attended_near = lax.dynamic_slice_in_dim(attended, core * width, width, 1)
            attended_far = lax.dynamic_slice_in_dim(attended, (1 - core) * width, width, 1)
            share_other = jnp.dot(attended_near, out_near, preferred_element_type=jnp.float32)
            share_other += jnp.dot(attended_far, out_far, preferred_element_type=jnp.float32)
            mine = scattered(share_mine.astype(jnp.bfloat16)).reshape(chunk, -1, out_half)
            other = scattered(share_other.astype(jnp.bfloat16)).reshape(chunk, -1, out_half)
            outs.append(
                jnp.where(
                    stream == 0, jnp.stack([mine, other], axis=2), jnp.stack([other, mine], axis=2)
                ).reshape(chunk, -1)
            )
    return jnp.concatenate(outs, axis=0).reshape(1, windows, frame_count, -1)


def solution(mesh):
    in_specs = (
        P("stream", None, "seq", "tensor"),
        P(),
        P("seq", "tensor"),
        P("seq", "tensor"),
        P("seq", "tensor"),
        P("tensor", "seq"),
    )
    out_specs = P("stream", None, "seq", "tensor")
    return jax.shard_map(body, mesh=mesh, in_specs=in_specs, out_specs=out_specs, check_vma=False)
```

```python
import functools

import jax
import jax.numpy as jnp
from jax import lax
from jax.experimental import pallas as pl
from jax.experimental.pallas import tpu as pltpu
from jax.sharding import PartitionSpec as P

HEAD_DIM = 128
ROW_CHUNKS = 2
KEY_BLOCK = 1024
LOG2E = 1.4426950408889634


def swap_pairs(block, axis):
    count = lax.axis_size(axis)
    return lax.ppermute(block, axis, [(i, i ^ 1) for i in range(count)])


def attend_kernel(repeat, start_ref, q_ref, k_ref, v_ref, o_ref, m_ref, l_ref, acc_ref):
    step = pl.program_id(1)
    rows = q_ref.shape[0]
    keys = k_ref.shape[0]
    start = start_ref[0]
    last = (start + rows - 1) // keys
    scale = LOG2E * HEAD_DIM ** (-0.5)

    @pl.when(step == 0)
    def _():
        m_ref[...] = jnp.full_like(m_ref, -1e30)
        l_ref[...] = jnp.zeros_like(l_ref)
        acc_ref[...] = jnp.zeros_like(acc_ref)

    def update(masked):
        k = k_ref[...]
        v = v_ref[...]
        if masked:
            frame = start + lax.broadcasted_iota(jnp.int32, (keys, rows), 1)
            key = step * keys + lax.broadcasted_iota(jnp.int32, (keys, rows), 0)
            allowed = key <= frame

        def scored(r):
            q = q_ref[:, r * HEAD_DIM:(r + 1) * HEAD_DIM]
            return lax.dot_general(k, q, (((1,), (1,)), ((), ())), preferred_element_type=jnp.float32)

        following = scored(0)
        for r in range(repeat):
            s = following
            if r + 1 < repeat:
                following = scored(r + 1)
            if masked:
                s = jnp.where(allowed, s, -1e30)
            top = jnp.max(s, axis=0, keepdims=True) * scale
            before = m_ref[r]
            fresh = jnp.maximum(before, top)
            m_ref[r] = fresh
            alpha = jnp.exp2(before - fresh)
            p = jnp.exp2(s * scale - fresh)
            l_ref[r] = alpha * l_ref[r] + jnp.sum(p, axis=0, keepdims=True)
            acc_ref[r] = alpha * acc_ref[r] + lax.dot_general(
                v, p.astype(jnp.bfloat16), (((0,), (0,)), ((), ())), preferred_element_type=jnp.float32
            )

    @pl.when(step < last)
    def _():
        update(False)

    @pl.when(step == last)
    def _():
        update(True)
        for r in range(repeat):
            attended = (acc_ref[r] / l_ref[r]).T
            o_ref[:, r * HEAD_DIM:(r + 1) * HEAD_DIM] = attended.astype(o_ref.dtype)


def attend(start, queries, keys_values, repeat):
    rows, width = queries.shape
    count = keys_values.shape[0]
    groups = width // (repeat * HEAD_DIM)
    block = min(KEY_BLOCK, count)

    def at(step, start_ref):
        return jnp.minimum(step, (start_ref[0] + rows - 1) // block)

    return pl.pallas_call(
        functools.partial(attend_kernel, repeat),
        out_shape=jax.ShapeDtypeStruct((rows, width), jnp.bfloat16),
        grid_spec=pltpu.PrefetchScalarGridSpec(
            num_scalar_prefetch=1,
            grid=(groups, count // block),
            in_specs=[
                pl.BlockSpec((rows, repeat * HEAD_DIM), lambda g, i, s: (0, g)),
                pl.BlockSpec((block, HEAD_DIM), lambda g, i, s: (at(i, s), g)),
                pl.BlockSpec((block, HEAD_DIM), lambda g, i, s: (at(i, s), groups + g)),
            ],
            out_specs=pl.BlockSpec((rows, repeat * HEAD_DIM), lambda g, i, s: (0, g)),
            scratch_shapes=[
                pltpu.VMEM((repeat, 1, rows), jnp.float32),
                pltpu.VMEM((repeat, 1, rows), jnp.float32),
                pltpu.VMEM((repeat, HEAD_DIM, rows), jnp.float32),
            ],
        ),
        compiler_params=pltpu.CompilerParams(
            dimension_semantics=("arbitrary", "arbitrary"), vmem_limit_bytes=32 * 1024 * 1024
        ),
        cost_estimate=pl.CostEstimate(
            flops=8 * rows * count * width,
            bytes_accessed=2 * (2 * rows * width + keys_values.size),
            transcendentals=rows * count * width // HEAD_DIM,
        ),
    )(start.reshape(1), queries, keys_values, keys_values)


def y_share(mine, core):
    depth = mine.shape[0] // 2
    part = lax.dynamic_slice_in_dim(mine, core * depth, depth, 0)
    near = lax.ppermute(part, "stream", [(0, 1), (1, 0)])
    far = swap_pairs(near, "seq")
    return near, far


def body(hidden, norm_gain, query_weight, key_weight, value_projection_weight, out_weight):
    windows, frame_count = hidden.shape[1], hidden.shape[2]
    n_tensor = lax.axis_size("tensor")
    n_seq = lax.axis_size("seq")
    stream = lax.axis_index("stream")
    tensor = lax.axis_index("tensor")
    seq = lax.axis_index("seq")
    core = seq % 2
    rows = windows * frame_count
    depth = query_weight.shape[0] // 2
    out_half = out_weight.shape[1] // 2

    kv_weight = jnp.concatenate([key_weight, value_projection_weight], axis=1)
    kv_mine = lax.all_gather(
        lax.dynamic_slice_in_dim(kv_weight, stream * depth, depth, 0), "seq", axis=0, tiled=True
    )
    query_mine = lax.all_gather(
        lax.dynamic_slice_in_dim(query_weight, stream * depth, depth, 0), "seq", axis=0, tiled=True
    )
    out_mine = lax.all_gather(
        lax.dynamic_slice_in_dim(out_weight, stream * out_half, out_half, 1), "seq", axis=1, tiled=True
    )

    local = hidden.reshape(rows, hidden.shape[3])
    if n_tensor == 2:
        other = lax.ppermute(local, "tensor", [(0, 1), (1, 0)])
        gathered = jnp.where(
            tensor == 0,
            jnp.concatenate([local, other], axis=1),
            jnp.concatenate([other, local], axis=1),
        )
    else:
        gathered = lax.all_gather(local, "tensor", axis=1, tiled=True)
    flat = gathered.astype(jnp.float32)
    inverse_rms = lax.rsqrt(jnp.mean(flat * flat, axis=1, keepdims=True) + 1e-05)
    normed = (flat * inverse_rms * norm_gain).astype(jnp.bfloat16)
    split = normed.reshape(rows, n_seq, 2, depth)

    def features(half):
        return lax.dynamic_index_in_dim(split, half, 2, keepdims=False).reshape(rows, n_seq * depth)

    normed_mine = features(stream)
    normed_other = features(1 - stream)
    span = n_seq * depth // 2
    normed_near = lax.dynamic_slice_in_dim(normed_other, core * span, span, 1)
    normed_far = lax.dynamic_slice_in_dim(normed_other, (1 - core) * span, span, 1)

    def project(mine, near, far):
        total = jnp.dot(normed_mine, mine, preferred_element_type=jnp.float32)
        total += jnp.dot(normed_near, near, preferred_element_type=jnp.float32)
        total += jnp.dot(normed_far, far, preferred_element_type=jnp.float32)
        return total.astype(jnp.bfloat16)

    keys_values = project(kv_mine, *y_share(kv_mine, core))
    partner = lax.ppermute(keys_values, "stream", [(0, 1), (1, 0)])
    kv_width = key_weight.shape[1]
    parts = 2 if kv_width % (2 * HEAD_DIM) == 0 else 1
    step = kv_width // parts
    pieces = []
    for part in range(parts):
        columns = jnp.concatenate(
            [partner[:, part * step:(part + 1) * step],
             partner[:, kv_width + part * step:kv_width + (part + 1) * step]],
            axis=1,
        )
        pieces.append(
            lax.all_gather(columns.reshape(windows, frame_count, 2 * step), "seq", axis=1, tiled=True)
        )
    queries = project(query_mine, *y_share(query_mine, core)).reshape(windows, frame_count, -1)
    out_near, out_far = y_share(out_mine, core)
    width = out_weight.shape[0] // 2

    repeat = query_weight.shape[1] // key_weight.shape[1]
    chunk = frame_count // ROW_CHUNKS

    def scattered(share):
        if n_tensor == 2:
            wide = share.shape[1] // 2
            away = lax.dynamic_slice_in_dim(share, (1 - tensor) * wide, wide, 1)
            kept = lax.dynamic_slice_in_dim(share, tensor * wide, wide, 1)
            came = lax.ppermute(away, "tensor", [(0, 1), (1, 0)])
            return (kept.astype(jnp.float32) + came.astype(jnp.float32)).astype(jnp.bfloat16)
        return lax.psum_scatter(share, "tensor", scatter_dimension=1, tiled=True)

    outs = []
    q_step = step * repeat
    for window in range(windows):
        early = [
            attend(
                seq * frame_count,
                queries[window][:, part * q_step:(part + 1) * q_step],
                pieces[part][window],
                repeat,
            )
            for part in range(parts - 1)
        ]
        for index in range(ROW_CHUNKS):
            low, high = index * chunk, (index + 1) * chunk
            final = attend(
                seq * frame_count + low,
                queries[window][low:high, (parts - 1) * q_step:],
                pieces[-1][window],
                repeat,
            )
            attended = jnp.concatenate([done[low:high] for done in early] + [final], axis=1)
            share_mine = jnp.dot(attended, out_mine, preferred_element_type=jnp.float32)
            attended_near = lax.dynamic_slice_in_dim(attended, core * width, width, 1)
            attended_far = lax.dynamic_slice_in_dim(attended, (1 - core) * width, width, 1)
            share_other = jnp.dot(attended_near, out_near, preferred_element_type=jnp.float32)
            share_other += jnp.dot(attended_far, out_far, preferred_element_type=jnp.float32)
            mine = scattered(share_mine.astype(jnp.bfloat16)).reshape(chunk, -1, out_half)
            other = scattered(share_other.astype(jnp.bfloat16)).reshape(chunk, -1, out_half)
            outs.append(
                jnp.where(
                    stream == 0, jnp.stack([mine, other], axis=2), jnp.stack([other, mine], axis=2)
                ).reshape(chunk, -1)
            )
    return jnp.concatenate(outs, axis=0).reshape(1, windows, frame_count, -1)


def solution(mesh):
    in_specs = (
        P("stream", None, "seq", "tensor"),
        P(),
        P("seq", "tensor"),
        P("seq", "tensor"),
        P("seq", "tensor"),
        P("tensor", "seq"),
    )
    out_specs = P("stream", None, "seq", "tensor")
    return jax.shard_map(body, mesh=mesh, in_specs=in_specs, out_specs=out_specs, check_vma=False)
```

```python
import functools

import jax
import jax.numpy as jnp
from jax import lax
from jax.experimental import pallas as pl
from jax.experimental.pallas import tpu as pltpu
from jax.sharding import PartitionSpec as P

HEAD_DIM = 128
ROW_CHUNKS = 2
KEY_BLOCK = 1024
LOG2E = 1.4426950408889634


def swap_pairs(block, axis):
    count = lax.axis_size(axis)
    return lax.ppermute(block, axis, [(i, i ^ 1) for i in range(count)])


def attend_kernel(repeat, start_ref, q_ref, k_ref, v_ref, o_ref, m_ref, l_ref, acc_ref):
    step = pl.program_id(1)
    rows = q_ref.shape[0]
    keys = k_ref.shape[0]
    start = start_ref[0]
    last = (start + rows - 1) // keys
    scale = LOG2E * HEAD_DIM ** (-0.5)

    @pl.when(step == 0)
    def _():
        m_ref[...] = jnp.full_like(m_ref, -1e30)
        l_ref[...] = jnp.zeros_like(l_ref)
        acc_ref[...] = jnp.zeros_like(acc_ref)

    def update(masked):
        k = k_ref[...]
        v = v_ref[...]
        if masked:
            frame = start + lax.broadcasted_iota(jnp.int32, (keys, rows), 1)
            key = step * keys + lax.broadcasted_iota(jnp.int32, (keys, rows), 0)
            allowed = key <= frame

        def scored(r):
            q = q_ref[:, r * HEAD_DIM:(r + 1) * HEAD_DIM]
            return lax.dot_general(k, q, (((1,), (1,)), ((), ())), preferred_element_type=jnp.float32)

        following = scored(0)
        for r in range(repeat):
            s = following
            if r + 1 < repeat:
                following = scored(r + 1)
            if masked:
                s = jnp.where(allowed, s, -1e30)
            top = jnp.max(s, axis=0, keepdims=True) * scale
            before = m_ref[r]
            fresh = jnp.maximum(before, top)
            m_ref[r] = fresh
            alpha = jnp.exp2(before - fresh)
            p = jnp.exp2(s * scale - fresh)
            l_ref[r] = alpha * l_ref[r] + jnp.sum(p, axis=0, keepdims=True)
            acc_ref[r] = alpha * acc_ref[r] + lax.dot_general(
                v, p.astype(jnp.bfloat16), (((0,), (0,)), ((), ())), preferred_element_type=jnp.float32
            )

    @pl.when(step < last)
    def _():
        update(False)

    @pl.when(step == last)
    def _():
        update(True)
        for r in range(repeat):
            attended = (acc_ref[r] / l_ref[r]).T
            o_ref[:, r * HEAD_DIM:(r + 1) * HEAD_DIM] = attended.astype(o_ref.dtype)


def attend(start, queries, keys_values, repeat):
    rows, width = queries.shape
    count = keys_values.shape[0]
    groups = width // (repeat * HEAD_DIM)
    block = min(KEY_BLOCK, count)

    def at(step, start_ref):
        return jnp.minimum(step, (start_ref[0] + rows - 1) // block)

    return pl.pallas_call(
        functools.partial(attend_kernel, repeat),
        out_shape=jax.ShapeDtypeStruct((rows, width), jnp.bfloat16),
        grid_spec=pltpu.PrefetchScalarGridSpec(
            num_scalar_prefetch=1,
            grid=(groups, count // block),
            in_specs=[
                pl.BlockSpec((rows, repeat * HEAD_DIM), lambda g, i, s: (0, g)),
                pl.BlockSpec((block, HEAD_DIM), lambda g, i, s: (at(i, s), g)),
                pl.BlockSpec((block, HEAD_DIM), lambda g, i, s: (at(i, s), groups + g)),
            ],
            out_specs=pl.BlockSpec((rows, repeat * HEAD_DIM), lambda g, i, s: (0, g)),
            scratch_shapes=[
                pltpu.VMEM((repeat, 1, rows), jnp.float32),
                pltpu.VMEM((repeat, 1, rows), jnp.float32),
                pltpu.VMEM((repeat, HEAD_DIM, rows), jnp.float32),
            ],
        ),
        compiler_params=pltpu.CompilerParams(
            dimension_semantics=("arbitrary", "arbitrary"), vmem_limit_bytes=32 * 1024 * 1024
        ),
        cost_estimate=pl.CostEstimate(
            flops=8 * rows * count * width,
            bytes_accessed=2 * (2 * rows * width + keys_values.size),
            transcendentals=rows * count * width // HEAD_DIM,
        ),
    )(start.reshape(1), queries, keys_values, keys_values)


def y_share(mine, core, after=None):
    depth = mine.shape[0] // 2
    part = lax.dynamic_slice_in_dim(mine, core * depth, depth, 0)
    near = lax.ppermute(part, "stream", [(0, 1), (1, 0)])
    if after is None:
        return near, swap_pairs(near, "seq")
    near, after = lax.optimization_barrier((near, after))
    return near, swap_pairs(near, "seq"), after


def body(hidden, norm_gain, query_weight, key_weight, value_projection_weight, out_weight):
    windows, frame_count = hidden.shape[1], hidden.shape[2]
    n_tensor = lax.axis_size("tensor")
    n_seq = lax.axis_size("seq")
    stream = lax.axis_index("stream")
    tensor = lax.axis_index("tensor")
    seq = lax.axis_index("seq")
    core = seq % 2
    rows = windows * frame_count
    depth = query_weight.shape[0] // 2
    out_half = out_weight.shape[1] // 2

    kv_weight = jnp.concatenate([key_weight, value_projection_weight], axis=1)
    kv_mine = lax.all_gather(
        lax.dynamic_slice_in_dim(kv_weight, stream * depth, depth, 0), "seq", axis=0, tiled=True
    )
    query_mine = lax.all_gather(
        lax.dynamic_slice_in_dim(query_weight, stream * depth, depth, 0), "seq", axis=0, tiled=True
    )
    out_mine = lax.all_gather(
        lax.dynamic_slice_in_dim(out_weight, stream * out_half, out_half, 1), "seq", axis=1, tiled=True
    )

    local = hidden.reshape(rows, hidden.shape[3])
    if n_tensor == 2:
        other = lax.ppermute(local, "tensor", [(0, 1), (1, 0)])
        gathered = jnp.where(
            tensor == 0,
            jnp.concatenate([local, other], axis=1),
            jnp.concatenate([other, local], axis=1),
        )
    else:
        gathered = lax.all_gather(local, "tensor", axis=1, tiled=True)
    flat = gathered.astype(jnp.float32)
    inverse_rms = lax.rsqrt(jnp.mean(flat * flat, axis=1, keepdims=True) + 1e-05)
    normed = (flat * inverse_rms * norm_gain).astype(jnp.bfloat16)
    split = normed.reshape(rows, n_seq, 2, depth)

    def features(half):
        return lax.dynamic_index_in_dim(split, half, 2, keepdims=False).reshape(rows, n_seq * depth)

    normed_mine = features(stream)
    normed_other = features(1 - stream)
    span = n_seq * depth // 2
    normed_near = lax.dynamic_slice_in_dim(normed_other, core * span, span, 1)
    normed_far = lax.dynamic_slice_in_dim(normed_other, (1 - core) * span, span, 1)

    def project(mine, near, far):
        total = jnp.dot(normed_mine, mine, preferred_element_type=jnp.float32)
        total += jnp.dot(normed_near, near, preferred_element_type=jnp.float32)
        total += jnp.dot(normed_far, far, preferred_element_type=jnp.float32)
        return total.astype(jnp.bfloat16)

    keys_values = project(kv_mine, *y_share(kv_mine, core))
    partner = lax.ppermute(keys_values, "stream", [(0, 1), (1, 0)])
    kv_width = key_weight.shape[1]
    parts = 2 if kv_width % (2 * HEAD_DIM) == 0 else 1
    step = kv_width // parts
    pieces = []
    for part in range(parts):
        columns = jnp.concatenate(
            [partner[:, part * step:(part + 1) * step],
             partner[:, kv_width + part * step:kv_width + (part + 1) * step]],
            axis=1,
        )
        pieces.append(
            lax.all_gather(columns.reshape(windows, frame_count, 2 * step), "seq", axis=1, tiled=True)
        )
    queries = project(query_mine, *y_share(query_mine, core)).reshape(windows, frame_count, -1)
    out_near = out_far = None
    width = out_weight.shape[0] // 2

    repeat = query_weight.shape[1] // key_weight.shape[1]
    chunk = frame_count // ROW_CHUNKS

    def scattered(share):
        if n_tensor == 2:
            wide = share.shape[1] // 2
            away = lax.dynamic_slice_in_dim(share, (1 - tensor) * wide, wide, 1)
            kept = lax.dynamic_slice_in_dim(share, tensor * wide, wide, 1)
            came = lax.ppermute(away, "tensor", [(0, 1), (1, 0)])
            return (kept.astype(jnp.float32) + came.astype(jnp.float32)).astype(jnp.bfloat16)
        return lax.psum_scatter(share, "tensor", scatter_dimension=1, tiled=True)

    outs = []
    q_step = step * repeat
    for window in range(windows):
        early = [
            attend(
                seq * frame_count,
                queries[window][:, part * q_step:(part + 1) * q_step],
                pieces[part][window],
                repeat,
            )
            for part in range(parts - 1)
        ]
        for index in range(ROW_CHUNKS):
            low, high = index * chunk, (index + 1) * chunk
            final = attend(
                seq * frame_count + low,
                queries[window][low:high, (parts - 1) * q_step:],
                pieces[-1][window],
                repeat,
            )
            attended = jnp.concatenate([done[low:high] for done in early] + [final], axis=1)
            share_mine = jnp.dot(attended, out_mine, preferred_element_type=jnp.float32)
            if out_near is None:
                out_near, out_far, attended = y_share(out_mine, core, attended)
            attended_near = lax.dynamic_slice_in_dim(attended, core * width, width, 1)
            attended_far = lax.dynamic_slice_in_dim(attended, (1 - core) * width, width, 1)
            share_other = jnp.dot(attended_near, out_near, preferred_element_type=jnp.float32)
            share_other += jnp.dot(attended_far, out_far, preferred_element_type=jnp.float32)
            mine = scattered(share_mine.astype(jnp.bfloat16)).reshape(chunk, -1, out_half)
            other = scattered(share_other.astype(jnp.bfloat16)).reshape(chunk, -1, out_half)
            outs.append(
                jnp.where(
                    stream == 0, jnp.stack([mine, other], axis=2), jnp.stack([other, mine], axis=2)
                ).reshape(chunk, -1)
            )
    return jnp.concatenate(outs, axis=0).reshape(1, windows, frame_count, -1)


def solution(mesh):
    in_specs = (
        P("stream", None, "seq", "tensor"),
        P(),
        P("seq", "tensor"),
        P("seq", "tensor"),
        P("seq", "tensor"),
        P("tensor", "seq"),
    )
    out_specs = P("stream", None, "seq", "tensor")
    return jax.shard_map(body, mesh=mesh, in_specs=in_specs, out_specs=out_specs, check_vma=False)
```
